512 devices in a mesh: dp: 16 (over y, x), expert: 32 (over z, core).
Axes of the slice: x: 4, y: 4, z: 16, core: 2. Of those that a mesh axis runs over, the one named last changes fastest.
Arguments:
- tokens: bfloat16 [65536, 512], P(('dp', 'expert')), may hold values from -6 to 6
- cotangent: bfloat16 [65536, 512], P(('dp', 'expert')), may hold values from -0.29882812 to 0.29882812
- labels: int32 [65536, 1], P(('dp', 'expert')), may hold values from 0 to 63; in each aligned block of 128 rows (0 to 127, 128 to 255, ...) at most 4 rows name the same one
- placement: int32 [64], replicated, may hold values from 0 to 63, each once
- mass: float32 [65536], P(('dp', 'expert')), may hold values from 0.1 to 10
- w_head: float32 [512, 16], replicated, may hold values from -0.25 to 0.25
- w_up: bfloat16 [64, 512, 2048], P('expert', None, 'dp'), may hold values from -0.25 to 0.25
- w_down: bfloat16 [64, 2048, 512], P('expert', 'dp'), may hold values from -0.125 to 0.125
- up_moment: bfloat16 [64, 512, 2048], P('expert', None, 'dp'), may hold values from -2 to 2
- up_square: bfloat16 [64, 512, 2048], P('expert', None, 'dp'), may hold values from 0.0099487305 to 1
- down_moment: bfloat16 [64, 2048, 512], P('expert', 'dp'), may hold values from -2 to 2
- down_square: bfloat16 [64, 2048, 512], P('expert', 'dp'), may hold values from 0.0099487305 to 1
Outputs:
- fine_precip: float32 [65536, 16], P(('dp', 'expert'))
- up_next: bfloat16 [64, 512, 2048], P('expert', None, 'dp')
- down_next: bfloat16 [64, 2048, 512], P('expert', 'dp')
- up_moment_next: bfloat16 [64, 512, 2048], P('expert', None, 'dp')
- up_square_next: bfloat16 [64, 512, 2048], P('expert', None, 'dp')
- down_moment_next: bfloat16 [64, 2048, 512], P('expert', 'dp')
- down_square_next: bfloat16 [64, 2048, 512], P('expert', 'dp')
The draws below stay inside these ranges and needn't reach their ends.
Inputs may be any that keep to these rules, and one draw needn't show every extreme that they name: `labels`: within each device's block of 128 rows no regime is named more than 4 times, and in every draw some regime is named exactly 4 times in some block; every regime is named somewhere. `placement`: each regime stands in exactly one expert slot.
All inputs are finite; a program needn't handle non-finite values.
Results may differ from the reference program's by a relative error of at most 0.0045.
Values may be sent and summed in bfloat16 or wider, within the bound.
A program may use at most 64 MiB of HBM per device.

```python
import math
import jax
import jax.numpy as jnp
import numpy as np
from jax import lax

D = 512
FF = 2048
PIX = 16
CAP = 4
TOK_DEV = 128
EXPERTS = 64
TOKENS = 65536
N_DP = 16
N_EXPERT = 32


def levels(rng, dims, split, smallest, largest):
    gain, own = 1.0, jax.random.fold_in(rng, 6)
    for dim, parts in split:
        heights = jnp.exp(jax.random.uniform(jax.random.fold_in(own, dim), (parts,), jnp.float32, smallest / len(split), largest / len(split)))
        gain = gain * jnp.repeat(heights, dims[dim] // parts).reshape([-1 if axis == dim else 1 for axis in range(len(dims))])
    return gain


def routed_block(rng, own, number, rows, number_of, top, reach, skew):
    ranking = jax.random.permutation(rng, number_of)
    packed, common = portions_of(number_of, rows * top, reach, skew, True), portions_of(number_of, rows * top, reach, skew, False)
    places = jnp.arange(number_of)

    def named(sizes, rotation):
        used = int((sizes > 0).sum())
        fixed = max(1, used // 4)
        moved = fixed + (places - fixed + rotation * (used - fixed)) % max(1, number_of - fixed)
        return jnp.zeros((number_of,), jnp.int32).at[ranking[jnp.where(places < fixed, places, moved)]].set(jnp.asarray(sizes, jnp.int32))

    sizes = jnp.where(number % 4 == 0, named(packed, number // 4), named(common, number - number // 4 - 1))
    mixed = jax.random.permutation(jax.random.fold_in(own, 3), number_of)
    source_of, taker = mixed[0:number_of // 2 * 2:2], mixed[1:number_of // 2 * 2:2]
    room = jnp.minimum(sizes[source_of] - 1, reach - sizes[taker]) // 2
    room = jnp.where((source_of == ranking[0]) | (taker == ranking[0]) | (sizes[taker] == 0), 0, jnp.maximum(room, 0))
    moved = jax.random.randint(jax.random.fold_in(own, 4), (number_of // 2,), 0, 1 << 20) % (room + 1)
    sizes = sizes.at[source_of].add(-moved).at[taker].add(moved)
    members = jnp.searchsorted(jnp.cumsum(sizes), jnp.arange(rows * top), side="right").astype(jnp.int32)
    table = members.reshape(top, rows).T
    table = table[jax.random.permutation(jax.random.fold_in(own, 1), rows)]
    rotation = jax.random.randint(jax.random.fold_in(own, 2), (rows, 1), 0, top)
    return jnp.take_along_axis(table, (jnp.arange(top)[None, :] + rotation) % top, axis=1)


def portions_of(count, total, reach, skew, full):
    portions = [(1 << 20) // math.isqrt(grade ** skew) + 1 for grade in range(1, count + 1)]
    largest = reach if full else min(reach, max(-(-total // count), total * portions[0] // sum(portions)))
    least = 1 if total - largest >= count - 1 else 0
    counts, spare = [largest] + [least] * (count - 1), total - largest - least * (count - 1)
    while spare > 0:
        candidates = [i for i in range(1, count) if counts[i] < largest] or [i for i in range(1, count) if counts[i] < reach]
        pool, remaining = sum([portions[i] for i in candidates]), spare
        for i in candidates:
            more = min(reach - counts[i], max(1, remaining * portions[i] // pool), spare)
            counts[i] = counts[i] + more
            spare = spare - more
    return np.array(counts)


def gaussian(own_key, dims, deviation, reach, cuts=(), held_as=jnp.bfloat16):
    result = jax.random.normal(own_key, dims, jnp.float32) * deviation
    if len(cuts) > 0:
        result = levels(own_key, dims, cuts, -0.22, 0.18) * result
    return jnp.clip(result, min=-reach, max=reach).astype(held_as)


def setup_inputs(seed: int = 0) -> dict:
    splits = jax.random.split(jax.random.key(seed), 13)
    tokens = gaussian(splits[0], (TOKENS, D), 1.0, 6.0, ((0, 512),))
    cotangent = gaussian(splits[1], (TOKENS, D), 0.05, 0.29882812, ((0, 512),))
    labels_keys = jax.random.split(jax.random.fold_in(splits[2], 1), TOKENS // TOK_DEV)
    labels_turns = jax.random.permutation(jax.random.fold_in(splits[2], 3), TOKENS // TOK_DEV)
    labels = jax.vmap(lambda own, number: routed_block(jax.random.fold_in(splits[2], 2), own, number, TOK_DEV, EXPERTS, 1, CAP, 2))(labels_keys, labels_turns).reshape((TOKENS, 1))
    placement = jax.random.permutation(splits[3], EXPERTS).astype(jnp.int32)
    mass = jnp.clip(jnp.exp(math.log(10.0) - 4.6051702 * jax.random.uniform(splits[4], (TOKENS,), jnp.float32) ** levels(splits[4], (TOKENS,), ((0, 512),), -0.2, 0.2)), 0.1, 10.0)
    w_head = gaussian(splits[5], (D, PIX), D ** -0.5, 0.25, (), jnp.float32)
    w_up = gaussian(splits[6], (EXPERTS, D, FF), D ** -0.5, 0.25, ((0, 32), (2, 16)))
    w_down = gaussian(splits[7], (EXPERTS, FF, D), FF ** -0.5, 0.125, ((0, 32), (1, 16)))
    up_moment = gaussian(splits[8], (EXPERTS, D, FF), 0.3, 2.0, ((0, 32), (2, 16)))
    up_square = jnp.clip(jnp.exp(math.log(1.0) - 4.61031033 * jax.random.uniform(splits[9], (EXPERTS, D, FF), jnp.float32) ** levels(splits[9], (EXPERTS, D, FF), ((0, 32), (2, 16)), -0.2, 0.2)), 0.0099487305, 1.0).astype(jnp.bfloat16)
    down_moment = gaussian(splits[10], (EXPERTS, FF, D), 0.3, 2.0, ((0, 32), (1, 16)))
    down_square = jnp.clip(jnp.exp(math.log(1.0) - 4.61031033 * jax.random.uniform(splits[11], (EXPERTS, FF, D), jnp.float32) ** levels(splits[11], (EXPERTS, FF, D), ((0, 32), (1, 16)), -0.2, 0.2)), 0.0099487305, 1.0).astype(jnp.bfloat16)
    return {"tokens": tokens, "cotangent": cotangent, "labels": labels, "placement": placement, "mass": mass, "w_head": w_head, "w_up": w_up, "w_down": w_down, "up_moment": up_moment, "up_square": up_square, "down_moment": down_moment, "down_square": down_square}


beta_first = 0.9
beta_second = 0.95
correct_first = 1.0 - 0.9 ** 20
correct_second = 1.0 - 0.95 ** 20
learn_rate = 0.002
adam_epsilon = 1e-08

def gelu_parts(pre):
    normal_cdf = 0.5 * (1.0 + lax.erf(pre * 0.7071067811865476))
    density = jnp.exp(-0.5 * pre * pre) * 0.3989422804014327
    return (pre * normal_cdf, normal_cdf + pre * density)

def adam_step(weight, first, second, grad):
    new_first = beta_first * first.astype(jnp.float32) + (1.0 - beta_first) * grad
    new_second = beta_second * second.astype(jnp.float32) + (1.0 - beta_second) * grad * grad
    update = new_first / correct_first / (jnp.sqrt(new_second / correct_second) + adam_epsilon)
    moved = weight.astype(jnp.float32) - learn_rate * update
    return (moved.astype(jnp.bfloat16), new_first.astype(jnp.bfloat16), new_second.astype(jnp.bfloat16))

def reference(tokens, cotangent, labels, placement, mass, w_head, w_up, w_down, up_moment, up_square, down_moment, down_square):
    experts = placement.shape[0]
    total = tokens.shape[0]
    width = tokens.shape[1]
    regimes = jnp.arange(experts, dtype=jnp.int32)
    owner = lax.optimization_barrier(jnp.sum(jnp.where(placement[None, :] == regimes[:, None], regimes[None, :], 0), axis=1)).astype(jnp.int32)
    slot_of = jnp.take(owner, labels[:, 0].astype(jnp.int32), axis=0).astype(jnp.int32)
    limit = N_DP * N_EXPERT * CAP
    share = FF // N_DP
    padded_x = jnp.concatenate([tokens, jnp.zeros((1, width), jnp.bfloat16)], axis=0)
    padded_grad = jnp.concatenate([cotangent, jnp.zeros((1, width), jnp.bfloat16)], axis=0)

    def per_expert(carry, inputs):
        slot, w_in, w_out, in_first, in_second, out_first, out_second = inputs
        rows_index = jnp.nonzero(slot_of == slot, size=limit, fill_value=total)[0].astype(jnp.int32)
        x_rows = jnp.take(padded_x, rows_index, axis=0)
        grad_rows = jnp.take(padded_grad, rows_index, axis=0)
        pre = jnp.dot(x_rows, w_in, preferred_element_type=jnp.float32)
        value, slope = gelu_parts(pre)
        hidden = value.astype(jnp.bfloat16)
        summed = jnp.zeros((limit, width), jnp.float32)
        for part in range(N_DP):
            term = jnp.dot(hidden[:, part * share:(part + 1) * share], w_out[part * share:(part + 1) * share], preferred_element_type=jnp.float32)
            summed = summed + lax.optimization_barrier(term.astype(jnp.bfloat16)).astype(jnp.float32)
        out_rows = summed.astype(jnp.bfloat16)
        back = lax.dot_general(grad_rows, w_out, (((1,), (1,)), ((), ())), preferred_element_type=jnp.float32)
        hidden_grad = (back * slope).astype(jnp.bfloat16)
        grad_in = lax.dot_general(x_rows, hidden_grad, (((0,), (0,)), ((), ())), preferred_element_type=jnp.float32)
        grad_out = lax.dot_general(hidden, grad_rows, (((0,), (0,)), ((), ())), preferred_element_type=jnp.float32)
        in_next = adam_step(w_in, in_first, in_second, grad_in)
        out_next = adam_step(w_out, out_first, out_second, grad_out)
        carry = carry.at[rows_index].set(out_rows)
        return (carry, (in_next[0], out_next[0], in_next[1], in_next[2], out_next[1], out_next[2]))
    start = jnp.zeros((total + 1, width), jnp.bfloat16)
    gathered, results = lax.scan(per_expert, start, (regimes, w_up, w_down, up_moment, up_square, down_moment, down_square))
    expert_out = gathered[:total]
    field = tokens.astype(jnp.float32) + expert_out.astype(jnp.float32)
    logits = jnp.dot(field, w_head, precision=lax.Precision.HIGHEST, preferred_element_type=jnp.float32)
    positive = jax.nn.softplus(logits) + 0.1
    fine_precip = mass[:, None] * positive / lax.optimization_barrier(jnp.sum(positive, axis=1, keepdims=True))
    return (fine_precip, results[0], results[1], results[2], results[3], results[4], results[5])
```

```python
import functools

import jax
import jax.numpy as jnp
from jax import lax
from jax.experimental import pallas as pl
from jax.experimental.pallas import tpu as pltpu
from jax.sharding import PartitionSpec as P

MESH = pl.DeviceIdType.MESH
F32 = jnp.float32
BF16 = jnp.bfloat16

CAP = 4
NX = 4
NY = 4

beta_first = 0.9
beta_second = 0.95
correct_first = 1.0 - 0.9**20
correct_second = 1.0 - 0.95**20
learn_rate = 0.002
adam_epsilon = 1e-08


def gelu_parts(pre):
    normal_cdf = 0.5 * (1.0 + lax.erf(pre * 0.7071067811865476))
    density = jnp.exp(-0.5 * pre * pre) * 0.3989422804014327
    return (pre * normal_cdf, normal_cdf + pre * density)


def adam_step(weight, first, second, grad):
    new_first = beta_first * first.astype(F32) + (1.0 - beta_first) * grad
    new_second = beta_second * second.astype(F32) + (1.0 - beta_second) * grad * grad
    update = new_first / correct_first / (jnp.sqrt(new_second / correct_second) + adam_epsilon)
    moved = weight.astype(F32) - learn_rate * update
    return moved.astype(BF16), new_first.astype(BF16), new_second.astype(BF16)


def dot(a, b, contract=((1,), (0,))):
    return lax.dot_general(a, b, (contract, ((), ())), preferred_element_type=F32)


def kernel(
    nz,
    tok_ref, cot_ref, lab_ref, plc_ref, mass_ref, head_ref,
    wup_ref, wdn_ref, um_ref, us_ref, dm_ref, ds_ref,
    fine_ref, upn_ref, dnn_ref, umn_ref, usn_ref, dmn_ref, dsn_ref,
    st_ref, zsrc, zbuf, ysrc, xbuf, wup, wdn, hid, slope, hg, part, rsbuf,
    ysend, yret, zsend, zret, gs_up, gs_dn, gr_up, gr_dn, gy_up, gy_dn, gf_up, gf_dn,
    w_send, w_recv, z_send, z_recv, y_send, y_recv, x_send, x_recv,
    rs_send, rs_recv, g_send, g_recv, gy_send, gy_recv,
):
    dp = lax.axis_index("dp")
    ex = lax.axis_index("expert")
    y, x = dp // NX, dp % NX
    z, c = ex // 2, ex % 2
    tokens, width = tok_ref.shape
    group = wup_ref.shape[2]
    slots = nz * NY * CAP
    rows = nz * CAP
    chunk = NY * rows

    def at(yy=None, xx=None, zz=None, cc=None):
        yy = y if yy is None else yy
        xx = x if xx is None else xx
        zz = z if zz is None else zz
        cc = c if cc is None else cc
        return (yy * NX + xx, zz * 2 + cc)

    def remote(src, dst, send, recv, device):
        return pltpu.make_async_remote_copy(
            src_ref=src, dst_ref=dst, send_sem=send, recv_sem=recv, device_id=device, device_id_type=MESH
        )

    barrier = pltpu.get_barrier_semaphore()

    def greet(i, carry):
        pl.semaphore_signal(barrier, inc=1, device_id=at(zz=(z + i) % nz), device_id_type=MESH)
        return carry

    lax.fori_loop(1, nz, greet, 0)
    for d in range(1, NX):
        pl.semaphore_signal(barrier, inc=1, device_id=at(xx=(x + d) % NX), device_id_type=MESH)
    for d in range(NY):
        if d > 0:
            pl.semaphore_signal(barrier, inc=1, device_id=at(yy=(y + d) % NY), device_id_type=MESH)
        pl.semaphore_signal(barrier, inc=1, device_id=at(yy=(y + d) % NY, cc=1 - c), device_id_type=MESH)

    chosen = lab_ref[...] == plc_ref[...]
    onehot = jnp.where(chosen, 1.0, 0.0).astype(F32)
    row = lax.broadcasted_iota(jnp.int32, (tokens, tokens), 0)
    col = lax.broadcasted_iota(jnp.int32, (tokens, tokens), 1)
    below = jnp.where(col < row, 1.0, 0.0).astype(BF16)
    earlier = dot(below, onehot.astype(BF16))
    first_slot = lax.broadcasted_iota(jnp.int32, onehot.shape, 1).astype(F32) * float(CAP)
    slot = jnp.sum(onehot * (earlier + first_slot), axis=1, keepdims=True).astype(jnp.int32)
    st = jnp.where(slot == lax.broadcasted_iota(jnp.int32, (tokens, slots), 1), 1.0, 0.0).astype(BF16)
    st_ref[...] = st

    def fill(kind, values):
        sent = dot(st_ref[...], values, ((0,), (0,))).astype(BF16)
        zsrc[kind] = sent.reshape(nz, NY * CAP, width)

    out_row = lax.broadcasted_iota(jnp.int32, (slots, slots), 0)
    in_row = lax.broadcasted_iota(jnp.int32, (slots, slots), 1)
    a_y, a_z, a_s = out_row // rows, (out_row // CAP) % nz, out_row % CAP
    swap = jnp.where(in_row == a_z * (NY * CAP) + a_y * CAP + a_s, 1.0, 0.0).astype(BF16)

    def z_copy(src, dst, k, d):
        zz = (z + d) % nz
        return remote(src.at[zz], dst.at[z], z_send.at[k, d], z_recv.at[k, d], at(zz=zz))

    def z_local(src, dst, k):
        return pltpu.make_async_copy(src.at[z], dst.at[z], z_recv.at[k, 0])

    def z_start(src, dst, k):
        def body(i, carry):
            half = (i + 1) // 2
            d = jnp.where(i % 2 == 1, nz // 2 - half, nz // 2 + half)
            z_copy(src, dst, k, d).start()
            return carry

        lax.fori_loop(0, nz - 1, body, 0)
        z_local(src, dst, k).start()

    def z_wait(src, dst, k):
        z_local(src, dst, k).wait()

        def body(d, carry):
            zz = (z + nz - d) % nz
            remote(src.at[zz], dst.at[zz], z_send.at[k, d], z_recv.at[k, d], at(zz=zz)).wait_recv()
            return carry

        lax.fori_loop(1, nz, body, 0)

    def z_sent(src, dst, k):
        def body(d, carry):
            z_copy(src, dst, k, d).wait_send()
            return carry

        lax.fori_loop(1, nz, body, 0)

    fill(0, tok_ref[...])
    pl.semaphore_wait(barrier, (nz - 1) + (NX - 1) + (NY - 1) + NY)
    z_start(zsrc.at[0], zbuf.at[0], 0)

    def w_pair(s, cc):
        yy = 2 * c + s
        pairs = (
            (wup_ref.at[s], wup.at[:, pl.ds(pl.multiple_of(y * group, group), group)]),
            (wdn_ref.at[s], wdn.at[pl.ds(pl.multiple_of(y * group, group), group)]),
        )
        here = jnp.logical_and(yy == y, cc == c)
        far = [
            remote(src, dst, w_send.at[s, cc, i], w_recv.at[y, i], at(yy=yy, cc=cc))
            for i, (src, dst) in enumerate(pairs)
        ]
        near = [pltpu.make_async_copy(src, dst, w_recv.at[y, i]) for i, (src, dst) in enumerate(pairs)]
        return here, near, far

    for s in range(2):
        for cc in range(2):
            here, near, far = w_pair(s, cc)

            @pl.when(here)
            def _():
                for copy in near:
                    copy.start()

            @pl.when(jnp.logical_not(here))
            def _():
                for copy in far:
                    copy.start()

    fill(1, cot_ref[...])
    z_start(zsrc.at[1], zbuf.at[1], 1)

    def y_copies(src, dst, k):
        return [
            remote(src.at[(y + d) % NY], dst.at[y], y_send.at[k, d], y_recv.at[k, d], at(yy=(y + d) % NY))
            for d in (2, 1, 3)
        ]

    def y_local(src, dst, k):
        return pltpu.make_async_copy(src.at[y], dst.at[y], y_recv.at[k, 0])

    def y_start(src, dst, k):
        for copy in y_copies(src, dst, k):
            copy.start()
        y_local(src, dst, k).start()

    def y_wait(src, dst, k):
        for d in (1, 3, 2):
            yy = (y + NY - d) % NY
            remote(src.at[yy], dst.at[yy], y_send.at[k, d], y_recv.at[k, d], at(yy=yy)).wait_recv()
        y_local(src, dst, k).wait()

    def y_sent(src, dst, k):
        for copy in y_copies(src, dst, k):
            copy.wait_send()

    right, left, across = (x + 1) % NX, (x + 3) % NX, (x + 2) % NX

    def to_y(k):
        z_wait(zsrc.at[k], zbuf.at[k], k)
        moved = dot(swap, zbuf[k].reshape(slots, width)).astype(BF16)
        ysrc[k] = moved.reshape(NY, rows, width)
        y_start(ysrc.at[k], xbuf.at[k, x], k)

    def x_copy(k, way, step, mine=True):
        half = NY // 2
        if step == 0:
            block = xbuf.at[k, x if mine else (left if way == 0 else right)]
        elif way == 0:
            block = xbuf.at[k, left if mine else across, 0:half]
        else:
            block = xbuf.at[k, right if mine else across, half:NY]
        return remote(
            block, block, x_send.at[k, way, step], x_recv.at[k, way, step], at(xx=right if way == 0 else left)
        )

    def to_x(k):
        y_wait(ysrc.at[k], xbuf.at[k, x], k)
        x_copy(k, 0, 0).start()
        x_copy(k, 1, 0).start()

    def pass_on(k):
        x_copy(k, 0, 0, False).wait_recv()
        x_copy(k, 0, 1).start()
        x_copy(k, 1, 0, False).wait_recv()
        x_copy(k, 1, 1).start()

    def last_x(k):
        x_copy(k, 0, 1, False).wait_recv()
        x_copy(k, 1, 1, False).wait_recv()

    half_width = wup.shape[1] // 2

    def forward(b):
        block = xbuf[0, b].reshape(chunk, width)
        pre = dot(block, wup[...])
        value, grad = gelu_parts(pre)
        slope[b] = grad
        hidden = value.astype(BF16)
        for h in range(2):
            hid[h, b] = hidden[:, h * half_width : (h + 1) * half_width]
        part[b] = dot(hidden, wdn[...]).astype(BF16)

    def backward(b):
        block = xbuf[1, b].reshape(chunk, width)
        back = dot(block, wdn[...], ((1,), (1,)))
        grad = (back * slope[b]).astype(BF16)
        for h in range(2):
            hg[h, b] = grad[:, h * half_width : (h + 1) * half_width]

    def rs_copy(d):
        xx = (x + d) % NX
        return remote(part.at[xx], rsbuf.at[d - 1], rs_send.at[d], rs_recv.at[d], at(xx=xx))

    to_y(0)
    to_x(0)
    for yy in range(NY):
        pltpu.make_async_copy(wup_ref.at[0], wup.at[:, yy * group : (yy + 1) * group], w_recv.at[yy, 0]).wait()
        pltpu.make_async_copy(wdn_ref.at[0], wdn.at[yy * group : (yy + 1) * group], w_recv.at[yy, 1]).wait()
    forward(x)
    pass_on(0)
    forward(right)
    rs_copy(1).start()
    forward(left)
    rs_copy(3).start()
    to_y(1)
    last_x(0)
    forward(across)
    rs_copy(2).start()
    to_x(1)
    backward(x)
    total = part[x].astype(F32)
    for d in (1, 3, 2):
        rs_copy(d).wait_recv()
        total = total + rsbuf[d - 1].astype(F32)
    ysend[...] = total.astype(BF16).reshape(NY, rows, width)
    y_start(ysend, yret, 2)
    pass_on(1)
    backward(right)
    backward(left)
    y_wait(ysend, yret, 2)
    back_row = lax.broadcasted_iota(jnp.int32, (slots, slots), 0)
    from_row = lax.broadcasted_iota(jnp.int32, (slots, slots), 1)
    b_z, b_y, b_s = back_row // (NY * CAP), (back_row // CAP) % NY, back_row % CAP
    unswap = jnp.where(from_row == b_y * rows + b_z * CAP + b_s, 1.0, 0.0).astype(BF16)
    moved = dot(unswap, yret[...].reshape(slots, width)).astype(BF16)
    zsend[...] = moved.reshape(nz, NY * CAP, width)
    z_start(zsend, zret, 2)
    last_x(1)
    backward(across)

    everything = NX * chunk
    flat_x = xbuf[0].reshape(everything, width)
    flat_c = xbuf[1].reshape(everything, width)

    def grads(h):
        up = dot(flat_x, hg[h].reshape(everything, half_width), ((0,), (0,)))
        down = dot(hid[h].reshape(everything, half_width), flat_c, ((0,), (0,)))
        return up, down

    up, down = grads(1 - c)
    gs_up[...] = up
    gs_dn[...] = down
    swap_up = remote(gs_up, gr_up, g_send.at[0], g_recv.at[0], at(cc=1 - c))
    swap_dn = remote(gs_dn, gr_dn, g_send.at[1], g_recv.at[1], at(cc=1 - c))
    swap_up.start()
    swap_dn.start()
    up, down = grads(c)
    swap_up.wait_recv()
    up = (up + gr_up[...]).astype(BF16)
    swap_dn.wait_recv()
    down = (down + gr_dn[...]).astype(BF16)
    owner, mine = y // 2, y % 2

    def gy_copies(k):
        yy = 2 * c + k
        gy_up[k] = up[:, k * group : (k + 1) * group]
        gy_dn[k] = down[k * group : (k + 1) * group]
        pairs = ((gy_up.at[k], gf_up.at[mine]), (gy_dn.at[k], gf_dn.at[mine]))
        far = [
            remote(src, dst, gy_send.at[k, i], gy_recv.at[mine, i], at(yy=yy, cc=owner))
            for i, (src, dst) in enumerate(pairs)
        ]
        near = [pltpu.make_async_copy(src, dst, gy_recv.at[mine, i]) for i, (src, dst) in enumerate(pairs)]
        return yy == y, near, far

    going = [gy_copies(k) for k in range(2)]
    for here, near, far in going:

        @pl.when(here)
        def _():
            for copy in near:
                copy.start()

        @pl.when(jnp.logical_not(here))
        def _():
            for copy in far:
                copy.start()

    z_wait(zsend, zret, 2)
    expert_out = dot(st_ref[...], zret[...].reshape(slots, width)).astype(BF16)
    field = tok_ref[...].astype(F32) + expert_out.astype(F32)
    logits = lax.dot_general(
        field, head_ref[...], (((1,), (0,)), ((), ())), precision=lax.Precision.HIGHEST, preferred_element_type=F32
    )
    positive = jnp.maximum(logits, 0.0) + jnp.log1p(jnp.exp(-jnp.abs(logits))) + 0.1
    mass = jnp.sum(jnp.where(row == col, mass_ref[...], 0.0), axis=1, keepdims=True)
    fine_ref[...] = mass * positive / jnp.sum(positive, axis=1, keepdims=True)

    for s in range(2):
        pltpu.make_async_copy(gy_up.at[0], gf_up.at[s], gy_recv.at[s, 0]).wait()
        upn_ref[s], umn_ref[s], usn_ref[s] = adam_step(wup_ref[s], um_ref[s], us_ref[s], gf_up[s].astype(F32))
        pltpu.make_async_copy(gy_dn.at[0], gf_dn.at[s], gy_recv.at[s, 1]).wait()
        dnn_ref[s], dmn_ref[s], dsn_ref[s] = adam_step(wdn_ref[s], dm_ref[s], ds_ref[s], gf_dn[s].astype(F32))

    for k in range(2):
        z_sent(zsrc.at[k], zbuf.at[k], k)
        y_sent(ysrc.at[k], xbuf.at[k, x], k)
        for way in range(2):
            for step in range(2):
                x_copy(k, way, step).wait_send()
    z_sent(zsend, zret, 2)
    y_sent(ysend, yret, 2)
    for d in range(1, NX):
        rs_copy(d).wait_send()
    swap_up.wait_send()
    swap_dn.wait_send()
    for s in range(2):
        for cc in range(2):
            here, near, far = w_pair(s, cc)

            @pl.when(jnp.logical_not(here))
            def _():
                for copy in far:
                    copy.wait_send()

    for here, near, far in going:

        @pl.when(jnp.logical_not(here))
        def _():
            for copy in far:
                copy.wait_send()


def local(
    tokens, cotangent, labels, placement, mass, w_head, w_up, w_down,
    up_moment, up_square, down_moment, down_square,
):
    nz = lax.axis_size("expert") // 2
    count, width = tokens.shape
    group = w_up.shape[2]
    full = NY * group
    slots = nz * NY * CAP
    rows = nz * CAP
    chunk = NY * rows
    vmem = pl.BlockSpec(memory_space=pltpu.VMEM)
    dma = pltpu.SemaphoreType.DMA
    shape = jax.ShapeDtypeStruct
    up_shape, down_shape = shape(w_up.shape, BF16), shape(w_down.shape, BF16)
    outs = pl.pallas_call(
        functools.partial(kernel, nz),
        out_shape=(
            shape((count, w_head.shape[1]), F32),
            up_shape, down_shape, up_shape, up_shape, down_shape, down_shape,
        ),
        in_specs=[vmem] * 12,
        out_specs=[vmem] * 7,
        scratch_shapes=[
            pltpu.VMEM((count, slots), BF16),
            pltpu.VMEM((2, nz, NY * CAP, width), BF16),
            pltpu.VMEM((2, nz, NY * CAP, width), BF16),
            pltpu.VMEM((2, NY, rows, width), BF16),
            pltpu.VMEM((2, NX, NY, rows, width), BF16),
            pltpu.VMEM((width, full), BF16),
            pltpu.VMEM((full, width), BF16),
            pltpu.VMEM((2, NX, chunk, full // 2), BF16),
            pltpu.VMEM((NX, chunk, full), F32),
            pltpu.VMEM((2, NX, chunk, full // 2), BF16),
            pltpu.VMEM((NX, chunk, width), BF16),
            pltpu.VMEM((NX - 1, chunk, width), BF16),
            pltpu.VMEM((NY, rows, width), BF16),
            pltpu.VMEM((NY, rows, width), BF16),
            pltpu.VMEM((nz, NY * CAP, width), BF16),
            pltpu.VMEM((nz, NY * CAP, width), BF16),
            pltpu.VMEM((width, full // 2), F32),
            pltpu.VMEM((full // 2, width), F32),
            pltpu.VMEM((width, full // 2), F32),
            pltpu.VMEM((full // 2, width), F32),
            pltpu.VMEM((2, width, group), BF16),
            pltpu.VMEM((2, group, width), BF16),
            pltpu.VMEM((2, width, group), BF16),
            pltpu.VMEM((2, group, width), BF16),
            dma((2, 2, 2)), dma((NY, 2)),
            dma((3, nz)), dma((3, nz)),
            dma((3, NY)), dma((3, NY)),
            dma((2, 2, 2)), dma((2, 2, 2)),
            dma((NX,)), dma((NX,)),
            dma((2,)), dma((2,)),
            dma((2, 2)), dma((2, 2)),
        ],
        compiler_params=pltpu.CompilerParams(
            collective_id=0, has_side_effects=True, vmem_limit_bytes=48 * 1024 * 1024
        ),
    )(
        tokens, cotangent, labels, placement[None, :], mass[None, :], w_head, w_up, w_down,
        up_moment, up_square, down_moment, down_square,
    )
    return tuple(outs)


def solution(mesh):
    by_token = P(("dp", "expert"), None)
    up, down = P("expert", None, "dp"), P("expert", "dp", None)
    return jax.shard_map(
        local,
        mesh=mesh,
        in_specs=(
            by_token, by_token, by_token, P(), P(("dp", "expert")), P(),
            up, down, up, up, down, down,
        ),
        out_specs=(by_token, up, down, up, up, down, down),
        check_vma=False,
    )
```

```python
import jax
import jax.numpy as jnp
from jax import lax
from jax.experimental import pallas as pl
from jax.experimental.pallas import tpu as pltpu
from jax.sharding import PartitionSpec as P

MESH = pl.DeviceIdType.MESH
F32 = jnp.float32
BF16 = jnp.bfloat16

CAP = 4
NX = 4
NY = 4
NZ = 16
SET = NZ // 2

beta_first = 0.9
beta_second = 0.95
correct_first = 1.0 - 0.9**20
correct_second = 1.0 - 0.95**20
learn_rate = 0.002
adam_epsilon = 1e-08


def gelu_parts(pre):
    normal_cdf = 0.5 * (1.0 + lax.erf(pre * 0.7071067811865476))
    density = jnp.exp(-0.5 * pre * pre) * 0.3989422804014327
    return (pre * normal_cdf, normal_cdf + pre * density)


def adam_step(weight, first, second, grad):
    new_first = beta_first * first.astype(F32) + (1.0 - beta_first) * grad
    new_second = beta_second * second.astype(F32) + (1.0 - beta_second) * grad * grad
    update = new_first / correct_first / (jnp.sqrt(new_second / correct_second) + adam_epsilon)
    moved = weight.astype(F32) - learn_rate * update
    return moved.astype(BF16), new_first.astype(BF16), new_second.astype(BF16)


def dot(a, b, contract=((1,), (0,))):
    return lax.dot_general(a, b, (contract, ((), ())), preferred_element_type=F32)


def kernel(
    tok_hbm, cot_hbm, lab_hbm, plc_hbm, mass_hbm, head_hbm, wup_ref, wdn_ref,
    fine_ref, gf_up, gf_dn,
    tok_ref, cot_ref, lab_ref, plc_ref, mass_ref, head_ref,
    ent_ref, ext_ref, to_rows, to_msgs, zsrc, zbuf, xbuf, wup, wdn, hid, slope, hg, part, rsbuf, zsend, zret, gs_up, gs_dn, gr_up, gr_dn, gy_up, gy_dn,
    in_sem, w_send, w_recv, ws_send, ws_recv, z_send, z_recv, x_send, x_recv,
    rs_send, rs_recv, g_send, g_recv, gy_send, gy_recv,
):
    dp = lax.axis_index("dp")
    ex = lax.axis_index("expert")
    y, x = dp // NX, dp % NX
    z, c = ex // 2, ex % 2
    tokens, width = tok_ref.shape
    group = wup_ref.shape[2]
    slots = NZ * NY * CAP
    count = SET * NY
    chunk = count * CAP
    message = zsrc.shape[2]
    lanes = zsrc.shape[3]
    quarters = width // lanes
    right, left, across = (x + 1) % NX, (x + 3) % NX, (x + 2) % NX

    def at(yy=None, xx=None, zz=None, cc=None):
        yy = y if yy is None else yy
        xx = x if xx is None else xx
        zz = z if zz is None else zz
        cc = c if cc is None else cc
        return (yy * NX + xx, zz * 2 + cc)

    def up_z(d):
        return z + d - jnp.where(z + d >= NZ, NZ, 0)

    def down_z(d):
        return z - d + jnp.where(z < d, NZ, 0)

    y_up = [(y + e) % NY for e in range(NY)]
    y_down = [y_up[(NY - e) % NY] for e in range(NY)]

    def remote(src, dst, send, recv, device):
        return pltpu.make_async_remote_copy(
            src_ref=src, dst_ref=dst, send_sem=send, recv_sem=recv, device_id=device, device_id_type=MESH
        )

    barrier = pltpu.get_barrier_semaphore()

    def greet(i, carry):
        for e in range(NY):
            pl.semaphore_signal(barrier, inc=1, device_id=at(yy=y_up[e], zz=up_z(i)), device_id_type=MESH)
        return carry

    inbound = [
        pltpu.make_async_copy(src, dst, in_sem.at[i])
        for i, (src, dst) in enumerate(
            (
                (lab_hbm, lab_ref), (plc_hbm, plc_ref), (tok_hbm, tok_ref),
                (cot_hbm, cot_ref), (mass_hbm, mass_ref), (head_hbm, head_ref),
            )
        )
    ]
    lax.fori_loop(1, NZ, greet, 0)
    for copy in inbound:
        copy.start()
    for d in range(1, NX):
        pl.semaphore_signal(barrier, inc=1, device_id=at(xx=(x + d) % NX), device_id_type=MESH)
    for e in range(NY):
        if e > 0:
            pl.semaphore_signal(barrier, inc=1, device_id=at(yy=y_up[e]), device_id_type=MESH)
        pl.semaphore_signal(barrier, inc=1, device_id=at(yy=y_up[e], cc=1 - c), device_id_type=MESH)

    def iota(shape, dim):
        return lax.broadcasted_iota(jnp.int32, shape, dim)

    def upright(value):
        size = value.shape[1]
        return jnp.sum(jnp.where(iota((size, size), 0) == iota((size, size), 1), value, 0), axis=1, keepdims=True)

    def one_hot(a, b):
        return jnp.where(a == b, 1.0, 0.0).astype(BF16)

    inbound[0].wait()
    inbound[1].wait()
    chosen = jnp.where(upright(plc_ref[...]) == lab_ref[...], 1.0, 0.0).astype(F32)
    before = jnp.where(iota((tokens, tokens), 0) < iota((tokens, tokens), 1), 1.0, 0.0).astype(BF16)
    earlier = dot(chosen.astype(BF16), before)
    first_slot = (iota(chosen.shape, 0) * CAP).astype(F32)
    slot = jnp.sum(chosen * (earlier + first_slot), axis=0, keepdims=True).astype(jnp.int32)
    key = jnp.concatenate([slot * quarters + q for q in range(quarters)], axis=1)

    def message_key(shape, dim):
        r = iota(shape, dim)
        return ((r // message) * CAP + r % CAP) * quarters + (r // CAP) % quarters

    ent_ref[...] = one_hot(message_key((slots * quarters, 1), 0), key)

    def stacked(value):
        return jnp.concatenate([value[:, q * lanes : (q + 1) * lanes] for q in range(quarters)], axis=0)

    def spread(value):
        size = value.shape[0] // quarters
        return jnp.concatenate([value[q * size : (q + 1) * size] for q in range(quarters)], axis=1)

    def fill(k, values):
        sent = dot(ent_ref[...], stacked(values)).astype(BF16)
        zsrc[k] = sent.reshape(NZ * NY, message, lanes)

    def prepare():
        size = chunk * quarters

        def place(shape, dim):
            r = iota(shape, dim)
            return ((r % chunk) // CAP) * message + (r // chunk) * CAP + r % CAP

        to_rows[...] = one_hot(place((size, 1), 0), iota((1, size), 1))
        to_msgs[...] = one_hot(iota((size, 1), 0), place((1, size), 1))
        columns = upright(slot)
        upright_key = jnp.concatenate([columns * quarters + q for q in range(quarters)], axis=0)
        ext_ref[...] = one_hot(upright_key, message_key((1, slots * quarters), 1))

    far_first, near_first = NZ // 2 - SET // 2 + 1, NZ - SET // 2 + 1
    self_index = NZ - near_first

    def z_loop(s, step, own):
        def all_y(d, j):
            for e in (2, 1, 3, 0):
                step(d, e, j * NY + e)

        def body(i, carry):
            if s == 0:
                all_y(far_first + i, i)
                all_y(far_first + SET - 1 - i, SET - 1 - i)
            else:
                all_y(near_first + i, i)
                all_y(self_index - i, 2 * self_index - i)
            return carry

        if s == 0:
            lax.fori_loop(0, SET // 2, body, 0)
        else:
            all_y(SET // 2, SET - 1)
            lax.fori_loop(0, self_index, body, 0)
            for e in (2, 1, 3):
                step(0, e, self_index * NY + e)
            own()

    def z_start(k, s):
        def step(d, e, i):
            zz, yy = up_z(d), y_up[e]
            remote(
                zsrc.at[k, zz * NY + yy], zbuf.at[k, s, i], z_send.at[k, s], z_recv.at[k, s], at(yy=yy, zz=zz)
            ).start()

        def local():
            pltpu.make_async_copy(
                zsrc.at[k, z * NY + y], zbuf.at[k, 1, self_index * NY], z_recv.at[k, 1]
            ).start()

        z_loop(s, step, local)

    def zr_start(s):
        def step(d, e, i):
            zz, yy = down_z(d), y_down[e]
            remote(
                zsend.at[s, i], zret.at[z * NY + y], z_send.at[2, s], z_recv.at[2, 0], at(yy=yy, zz=zz)
            ).start()

        def local():
            pltpu.make_async_copy(
                zsend.at[1, self_index * NY], zret.at[z * NY + y], z_recv.at[2, 0]
            ).start()

        z_loop(s, step, local)

    def z_wait(k, s):
        pltpu.make_async_copy(zbuf.at[k, s], zbuf.at[k, s], z_recv.at[k, s]).wait()

    def zr_wait():
        pltpu.make_async_copy(zret, zret, z_recv.at[2, 0]).wait()

    def z_sent(k, s):
        out = zsrc.at[0, 0 : count - s]
        pltpu.make_async_copy(out, out, z_send.at[k, s]).wait()

    inbound[2].wait()
    fill(0, tok_ref[...])
    pl.semaphore_wait(barrier, (NZ * NY - 1) + (NX - 1) + NY)
    z_start(0, 0)
    z_start(0, 1)

    def w_pair(s, i):
        yy = 2 * c + s
        piece = pl.ds(pl.multiple_of(y * group, group), group)
        src, dst = ((wup_ref.at[s], wup.at[:, piece]), (wdn_ref.at[s], wdn.at[piece]))[i]
        here = jnp.logical_and(yy == y, c == i)

        def far():
            return remote(src, dst, w_send.at[s, i], w_recv.at[y], at(yy=yy, cc=i))

        def near():
            return pltpu.make_async_copy(src, dst, w_recv.at[y])

        return here, near, far

    def w_start():
        for s in range(2):
            for i in range(2):
                here, near, far = w_pair(s, i)

                @pl.when(here)
                def _():
                    near().start()

                @pl.when(jnp.logical_not(here))
                def _():
                    far().start()

    def w_sent():
        for s in range(2):
            for i in range(2):
                here, near, far = w_pair(s, i)

                @pl.when(jnp.logical_not(here))
                def _():
                    far().wait_send()

    def w_share(i):
        ref = (wup, wdn)[i]
        return remote(ref, ref, ws_send.at[0], ws_recv.at[0], at(cc=1 - c))

    def w_pass():
        @pl.when(c == 0)
        def _():
            for yy in range(NY):
                pltpu.make_async_copy(wup_ref.at[0], wup.at[:, yy * group : (yy + 1) * group], w_recv.at[yy]).wait()
            w_share(0).start()

        @pl.when(c == 1)
        def _():
            for yy in range(NY):
                pltpu.make_async_copy(wdn_ref.at[0], wdn.at[yy * group : (yy + 1) * group], w_recv.at[yy]).wait()
            w_share(1).start()

    def w_done():
        @pl.when(c == 0)
        def _():
            w_share(1).wait_recv()
            w_share(0).wait_send()

        @pl.when(c == 1)
        def _():
            w_share(0).wait_recv()
            w_share(1).wait_send()

    w_start()
    inbound[3].wait()
    fill(1, cot_ref[...])

    middle = chunk // 2
    halves = (pl.ds(0, middle), pl.ds(middle, middle))

    def x_copy(k, s, way, step, mine=True):
        if step == 0:
            block = xbuf.at[k, s, x if mine else (left if way == 0 else right)]
        elif way == 0:
            block = xbuf.at[k, s, left if mine else across, halves[0]]
        else:
            block = xbuf.at[k, s, right if mine else across, halves[1]]
        return remote(
            block, block, x_send.at[k, s, way, step], x_recv.at[k, s, way, step],
            at(xx=right if way == 0 else left),
        )

    def to_x(k, s):
        z_wait(k, s)
        moved = dot(to_rows[...], zbuf[k, s].reshape(chunk * quarters, lanes)).astype(BF16)
        xbuf[k, s, x] = spread(moved)
        x_copy(k, s, 0, 0).start()
        x_copy(k, s, 1, 0).start()

    def pass_on(k, s):
        for way in range(2):
            x_copy(k, s, way, 0, False).wait_recv()
            x_copy(k, s, way, 1).start()

    def last_x(k, s):
        for way in range(2):
            x_copy(k, s, way, 1, False).wait_recv()

    def x_sent(k, s):
        for way in range(2):
            for step in range(2):
                x_copy(k, s, way, step).wait_send()

    half_width = wup.shape[1] // 2

    def forward(s, b):
        block = xbuf[0, s, b]
        value, grad = gelu_parts(dot(block, wup[...]))
        slope[s, b] = grad
        hidden = value.astype(BF16)
        for h in range(2):
            hid[h, s, b] = hidden[:, h * half_width : (h + 1) * half_width]
        part[s, b] = dot(hidden, wdn[...]).astype(BF16)

    def backward(s, b):
        block = xbuf[1, s, b]
        grad = (dot(block, wdn[...], ((1,), (1,))) * slope[s, b]).astype(BF16)
        for h in range(2):
            hg[h, s, b] = grad[:, h * half_width : (h + 1) * half_width]

    def rs_copy(s, d):
        xx = (x + d) % NX
        return remote(part.at[s, xx], rsbuf.at[s, d - 1], rs_send.at[s, d], rs_recv.at[s, d], at(xx=xx))

    def rs_sent(s):
        for d in range(1, NX):
            rs_copy(s, d).wait_send()

    def return_z(s):
        total = part[s, x].astype(F32)
        for d in (1, 3, 2):
            rs_copy(s, d).wait_recv()
            total = total + rsbuf[s, d - 1].astype(F32)
        moved = dot(to_msgs[...], stacked(total.astype(BF16))).astype(BF16)
        zsend[s] = moved.reshape(count, message, lanes)
        zr_start(s)

    everything = 2 * NX * chunk

    def grad_up(h):
        return dot(xbuf[0].reshape(everything, width), hg[h].reshape(everything, half_width), ((0,), (0,)))

    def grad_down(h):
        return dot(hid[h].reshape(everything, half_width), xbuf[1].reshape(everything, width), ((0,), (0,)))

    swap_up = remote(gs_up, gr_up, g_send.at[0], g_recv.at[0], at(cc=1 - c))
    swap_dn = remote(gs_dn, gr_dn, g_send.at[1], g_recv.at[1], at(cc=1 - c))
    owner, mine = y // 2, y % 2

    def gy_pair(k, i):
        yy = 2 * c + k
        src, dst = ((gy_up.at[k], gf_up.at[mine]), (gy_dn.at[k], gf_dn.at[mine]))[i]

        def far():
            return remote(src, dst, gy_send.at[k, i], gy_recv.at[mine, i], at(yy=yy, cc=owner))

        def near():
            return pltpu.make_async_copy(src, dst, gy_recv.at[mine, i])

        return yy == y, near, far

    def gy_start(i):
        for k in range(2):
            here, near, far = gy_pair(k, i)

            @pl.when(here)
            def _():
                near().start()

            @pl.when(jnp.logical_not(here))
            def _():
                far().start()

    def gy_sent(i):
        for k in range(2):
            here, near, far = gy_pair(k, i)

            @pl.when(jnp.logical_not(here))
            def _():
                far().wait_send()

    def gy_wait(i):
        src, dst = ((gy_up, gf_up), (gy_dn, gf_dn))[i]
        for s in range(2):
            pltpu.make_async_copy(src.at[0], dst.at[s], gy_recv.at[s, i]).wait()

    def head():
        zr_wait()
        expert_out = spread(dot(ext_ref[...], zret[...].reshape(slots * quarters, lanes)).astype(BF16))
        field = tok_ref[...].astype(F32) + expert_out.astype(F32)
        inbound[4].wait()
        inbound[5].wait()
        logits = lax.dot_general(
            head_ref[...], field, (((1,), (1,)), ((), ())), precision=lax.Precision.HIGHEST, preferred_element_type=F32
        )
        positive = jnp.maximum(logits, 0.0) + jnp.log1p(jnp.exp(-jnp.abs(logits))) + 0.1
        fine_ref[...] = mass_ref[...] * positive / jnp.sum(positive, axis=0, keepdims=True)

    def forward_near(s):
        forward(s, right)
        rs_copy(s, 1).start()
        forward(s, left)
        rs_copy(s, 3).start()

    def forward_far(s):
        forward(s, across)
        rs_copy(s, 2).start()

    prepare()
    to_x(0, 0)
    z_sent(0, 0)
    z_start(1, 0)
    w_pass()
    to_x(0, 1)
    z_sent(0, 1)
    z_start(1, 1)
    w_done()
    forward(0, x)
    pass_on(0, 0)
    forward(1, x)
    forward_near(0)
    pass_on(0, 1)
    last_x(0, 0)
    forward_far(0)
    forward_near(1)
    last_x(0, 1)
    forward_far(1)
    to_x(1, 0)
    return_z(0)
    backward(0, x)
    to_x(1, 1)
    pass_on(1, 0)
    return_z(1)
    backward(1, x)
    backward(0, right)
    backward(0, left)
    pass_on(1, 1)
    last_x(1, 0)
    backward(0, across)
    backward(1, right)
    backward(1, left)
    last_x(1, 1)
    gs_dn[...] = grad_down(1 - c)
    swap_dn.start()
    backward(1, across)
    gs_up[...] = grad_up(1 - c)
    swap_up.start()
    down = grad_down(c)
    swap_dn.wait_recv()
    down = (down + gr_dn[...]).astype(BF16)
    for k in range(2):
        gy_dn[k] = down[k * group : (k + 1) * group]
    gy_start(1)
    up = grad_up(c)
    swap_up.wait_recv()
    up = (up + gr_up[...]).astype(BF16)
    for k in range(2):
        gy_up[k] = up[:, k * group : (k + 1) * group]
    gy_start(0)
    head()
    gy_wait(1)
    gy_wait(0)

    for s in range(2):
        z_sent(1, s)
        z_sent(2, s)
        for k in range(2):
            x_sent(k, s)
        rs_sent(s)
    swap_up.wait_send()
    swap_dn.wait_send()
    gy_sent(0)
    gy_sent(1)
    w_sent()


def local(
    tokens, cotangent, labels, placement, mass, w_head, w_up, w_down,
    up_moment, up_square, down_moment, down_square,
):
    count, width = tokens.shape
    group = w_up.shape[2]
    full = NY * group
    slots = NZ * NY * CAP
    messages = SET * NY
    chunk = messages * CAP
    lanes = 128
    quarters = width // lanes
    message = quarters * CAP
    vmem = pl.BlockSpec(memory_space=pltpu.VMEM)
    hbm = pl.BlockSpec(memory_space=pl.ANY)
    dma = pltpu.SemaphoreType.DMA
    shape = jax.ShapeDtypeStruct
    pixels, experts = w_head.shape[1], placement.shape[0]
    fine, grad_up, grad_down = pl.pallas_call(
        kernel,
        out_shape=(shape((pixels, count), F32), shape(w_up.shape, BF16), shape(w_down.shape, BF16)),
        in_specs=[hbm] * 8,
        out_specs=[vmem] * 3,
        scratch_shapes=[
            pltpu.VMEM((count, width), BF16),
            pltpu.VMEM((count, width), BF16),
            pltpu.VMEM((1, count), jnp.int32),
            pltpu.VMEM((1, experts), jnp.int32),
            pltpu.VMEM((1, count), F32),
            pltpu.VMEM((pixels, width), F32),
            pltpu.VMEM((slots * quarters, count * quarters), BF16),
            pltpu.VMEM((count * quarters, slots * quarters), BF16),
            pltpu.VMEM((chunk * quarters, chunk * quarters), BF16),
            pltpu.VMEM((chunk * quarters, chunk * quarters), BF16),
            pltpu.VMEM((2, NZ * NY, message, lanes), BF16),
            pltpu.VMEM((2, 2, messages, message, lanes), BF16),
            pltpu.VMEM((2, 2, NX, chunk, width), BF16),
            pltpu.VMEM((width, full), BF16),
            pltpu.VMEM((full, width), BF16),
            pltpu.VMEM((2, 2, NX, chunk, full // 2), BF16),
            pltpu.VMEM((2, NX, chunk, full), F32),
            pltpu.VMEM((2, 2, NX, chunk, full // 2), BF16),
            pltpu.VMEM((2, NX, chunk, width), BF16),
            pltpu.VMEM((2, NX - 1, chunk, width), BF16),
            pltpu.VMEM((2, messages, message, lanes), BF16),
            pltpu.VMEM((NZ * NY, message, lanes), BF16),
            pltpu.VMEM((width, full // 2), F32),
            pltpu.VMEM((full // 2, width), F32),
            pltpu.VMEM((width, full // 2), F32),
            pltpu.VMEM((full // 2, width), F32),
            pltpu.VMEM((2, width, group), BF16),
            pltpu.VMEM((2, group, width), BF16),
            dma((6,)),
            dma((2, 2)), dma((NY,)),
            dma((1,)), dma((1,)),
            dma((3, 2)), dma((3, 2)),
            dma((2, 2, 2, 2)), dma((2, 2, 2, 2)),
            dma((2, NX)), dma((2, NX)),
            dma((2,)), dma((2,)),
            dma((2, 2)), dma((2, 2)),
        ],
        compiler_params=pltpu.CompilerParams(
            collective_id=0, has_side_effects=True, vmem_limit_bytes=56 * 1024 * 1024
        ),
    )(tokens, cotangent, labels.reshape(1, count), placement[None, :], mass[None, :], jnp.transpose(w_head), w_up, w_down)
    up = adam_step(w_up, up_moment, up_square, grad_up.astype(F32))
    down = adam_step(w_down, down_moment, down_square, grad_down.astype(F32))
    return jnp.transpose(fine), up[0], down[0], up[1], up[2], down[1], down[2]


def solution(mesh):
    by_token = P(("dp", "expert"), None)
    up, down = P("expert", None, "dp"), P("expert", "dp", None)
    return jax.shard_map(
        local,
        mesh=mesh,
        in_specs=(
            by_token, by_token, by_token, P(), P(("dp", "expert")), P(),
            up, down, up, up, down, down,
        ),
        out_specs=(by_token, up, down, up, up, down, down),
        check_vma=False,
    )
```

```python
import jax
import jax.numpy as jnp
from jax import lax
from jax.experimental import pallas as pl
from jax.experimental.pallas import tpu as pltpu
from jax.sharding import PartitionSpec as P

MESH = pl.DeviceIdType.MESH
F32 = jnp.float32
BF16 = jnp.bfloat16

CAP = 4
NX = 4
NY = 4
NZ = 16
SET = NZ // 2

beta_first = 0.9
beta_second = 0.95
correct_first = 1.0 - 0.9**20
correct_second = 1.0 - 0.95**20
learn_rate = 0.002
adam_epsilon = 1e-08


def gelu_parts(pre):
    normal_cdf = 0.5 * (1.0 + lax.erf(pre * 0.7071067811865476))
    density = jnp.exp(-0.5 * pre * pre) * 0.3989422804014327
    return (pre * normal_cdf, normal_cdf + pre * density)


def adam_step(weight, first, second, grad):
    new_first = beta_first * first.astype(F32) + (1.0 - beta_first) * grad
    new_second = beta_second * second.astype(F32) + (1.0 - beta_second) * grad * grad
    update = new_first / correct_first / (jnp.sqrt(new_second / correct_second) + adam_epsilon)
    moved = weight.astype(F32) - learn_rate * update
    return moved.astype(BF16), new_first.astype(BF16), new_second.astype(BF16)


def dot(a, b, contract=((1,), (0,))):
    return lax.dot_general(a, b, (contract, ((), ())), preferred_element_type=F32)


def kernel(
    tok_hbm, cot_hbm, lab_hbm, plc_hbm, mass_hbm, head_hbm, wup_ref, wdn_ref,
    fine_ref, gf_up, gf_dn,
    tok_ref, cot_ref, lab_ref, plc_ref, mass_ref, head_ref,
    ent_ref, ext_ref, to_rows, to_msgs, zsrc, zbuf, xbuf, wup, wdn, hid, slope, hg, part, rsbuf, zsend, zret, gs_up, gs_dn, gr_up, gr_dn, gy_up, gy_dn,
    in_sem, w_send, w_recv, ws_send, ws_recv, z_send, z_recv, x_send, x_recv,
    rs_send, rs_recv, g_send, g_recv, gy_send, gy_recv,
):
    dp = lax.axis_index("dp")
    ex = lax.axis_index("expert")
    y, x = dp // NX, dp % NX
    z, c = ex // 2, ex % 2
    tokens, width = tok_ref.shape
    group = wup_ref.shape[2]
    slots = NZ * NY * CAP
    count = SET * NY
    chunk = count * CAP
    message = zsrc.shape[2]
    lanes = zsrc.shape[3]
    quarters = width // lanes
    right, left, across = (x + 1) % NX, (x + 3) % NX, (x + 2) % NX

    def at(yy=None, xx=None, zz=None, cc=None):
        yy = y if yy is None else yy
        xx = x if xx is None else xx
        zz = z if zz is None else zz
        cc = c if cc is None else cc
        return (yy * NX + xx, zz * 2 + cc)

    def up_z(d):
        return z + d - jnp.where(z + d >= NZ, NZ, 0)

    def down_z(d):
        return z - d + jnp.where(z < d, NZ, 0)

    y_up = [(y + e) % NY for e in range(NY)]
    y_down = [y_up[(NY - e) % NY] for e in range(NY)]

    def remote(src, dst, send, recv, device):
        return pltpu.make_async_remote_copy(
            src_ref=src, dst_ref=dst, send_sem=send, recv_sem=recv, device_id=device, device_id_type=MESH
        )

    barrier = pltpu.get_barrier_semaphore()

    def greet(i, carry):
        for e in range(NY):
            pl.semaphore_signal(barrier, inc=1, device_id=at(yy=y_up[e], zz=up_z(i)), device_id_type=MESH)
        return carry

    inbound = [
        pltpu.make_async_copy(src, dst, in_sem.at[i])
        for i, (src, dst) in enumerate(
            (
                (lab_hbm, lab_ref), (plc_hbm, plc_ref), (tok_hbm, tok_ref),
                (cot_hbm, cot_ref), (mass_hbm, mass_ref), (head_hbm, head_ref),
            )
        )
    ]
    lax.fori_loop(1, NZ, greet, 0)
    for copy in inbound:
        copy.start()
    for d in range(1, NX):
        pl.semaphore_signal(barrier, inc=1, device_id=at(xx=(x + d) % NX), device_id_type=MESH)
    for e in range(NY):
        if e > 0:
            pl.semaphore_signal(barrier, inc=1, device_id=at(yy=y_up[e]), device_id_type=MESH)
        pl.semaphore_signal(barrier, inc=1, device_id=at(yy=y_up[e], cc=1 - c), device_id_type=MESH)

    def iota(shape, dim):
        return lax.broadcasted_iota(jnp.int32, shape, dim)

    def upright(value):
        size = value.shape[1]
        return jnp.sum(jnp.where(iota((size, size), 0) == iota((size, size), 1), value, 0), axis=1, keepdims=True)

    def one_hot(a, b):
        return jnp.where(a == b, 1.0, 0.0).astype(BF16)

    inbound[0].wait()
    inbound[1].wait()
    chosen = jnp.where(upright(plc_ref[...]) == lab_ref[...], 1.0, 0.0).astype(F32)
    before = jnp.where(iota((tokens, tokens), 0) < iota((tokens, tokens), 1), 1.0, 0.0).astype(BF16)
    earlier = dot(chosen.astype(BF16), before)
    first_slot = (iota(chosen.shape, 0) * CAP).astype(F32)
    slot = jnp.sum(chosen * (earlier + first_slot), axis=0, keepdims=True).astype(jnp.int32)
    key = jnp.concatenate([slot * quarters + q for q in range(quarters)], axis=1)

    def message_key(shape, dim):
        r = iota(shape, dim)
        return ((r // message) * CAP + r % CAP) * quarters + (r // CAP) % quarters

    ent_ref[...] = one_hot(message_key((slots * quarters, 1), 0), key)

    def stacked(value):
        return jnp.concatenate([value[:, q * lanes : (q + 1) * lanes] for q in range(quarters)], axis=0)

    def spread(value):
        size = value.shape[0] // quarters
        return jnp.concatenate([value[q * size : (q + 1) * size] for q in range(quarters)], axis=1)

    def fill(k, values):
        sent = dot(ent_ref[...], stacked(values)).astype(BF16)
        zsrc[k] = sent.reshape(NZ * NY, message, lanes)

    def prepare():
        size = chunk * quarters

        def place(shape, dim):
            r = iota(shape, dim)
            return ((r % chunk) // CAP) * message + (r // chunk) * CAP + r % CAP

        to_rows[...] = one_hot(place((size, 1), 0), iota((1, size), 1))
        to_msgs[...] = one_hot(iota((size, 1), 0), place((1, size), 1))
        columns = upright(slot)
        upright_key = jnp.concatenate([columns * quarters + q for q in range(quarters)], axis=0)
        ext_ref[...] = one_hot(upright_key, message_key((1, slots * quarters), 1))

    far_first, near_first = NZ // 2 - SET // 2 + 1, NZ - SET // 2 + 1
    self_index = NZ - near_first

    def z_loop(s, step, own):
        def all_y(d, j):
            for e in (2, 1, 3, 0):
                step(d, e, j * NY + e)

        def body(i, carry):
            if s == 0:
                all_y(far_first + i, i)
                all_y(far_first + SET - 1 - i, SET - 1 - i)
            else:
                all_y(near_first + i, i)
                all_y(self_index - i, 2 * self_index - i)
            return carry

        if s == 0:
            lax.fori_loop(0, SET // 2, body, 0)
        else:
            all_y(SET // 2, SET - 1)
            lax.fori_loop(0, self_index, body, 0)
            for e in (2, 1, 3):
                step(0, e, self_index * NY + e)
            own()

    def z_start(k, s):
        def step(d, e, i):
            zz, yy = up_z(d), y_up[e]
            remote(
                zsrc.at[k, zz * NY + yy], zbuf.at[k, s, i], z_send.at[k, s], z_recv.at[k, s], at(yy=yy, zz=zz)
            ).start()

        def local():
            pltpu.make_async_copy(
                zsrc.at[k, z * NY + y], zbuf.at[k, 1, self_index * NY], z_recv.at[k, 1]
            ).start()

        z_loop(s, step, local)

    def zr_start(s):
        def step(d, e, i):
            zz, yy = down_z(d), y_down[e]
            remote(
                zsend.at[s, i], zret.at[z * NY + y], z_send.at[2, s], z_recv.at[2, 0], at(yy=yy, zz=zz)
            ).start()

        def local():
            pltpu.make_async_copy(
                zsend.at[1, self_index * NY], zret.at[z * NY + y], z_recv.at[2, 0]
            ).start()

        z_loop(s, step, local)

    def z_wait(k, s):
        pltpu.make_async_copy(zbuf.at[k, s], zbuf.at[k, s], z_recv.at[k, s]).wait()

    def zr_wait():
        pltpu.make_async_copy(zret, zret, z_recv.at[2, 0]).wait()

    def z_sent(k, s):
        out = zsrc.at[0, 0 : count - s]
        pltpu.make_async_copy(out, out, z_send.at[k, s]).wait()

    inbound[2].wait()
    fill(0, tok_ref[...])
    pl.semaphore_wait(barrier, (NZ * NY - 1) + (NX - 1) + NY)
    z_start(0, 1)
    z_start(0, 0)

    def w_pair(s, i):
        yy = 2 * c + s
        piece = pl.ds(pl.multiple_of(y * group, group), group)
        src, dst = ((wup_ref.at[s], wup.at[:, piece]), (wdn_ref.at[s], wdn.at[piece]))[i]
        here = jnp.logical_and(yy == y, c == i)

        def far():
            return remote(src, dst, w_send.at[s, i], w_recv.at[y], at(yy=yy, cc=i))

        def near():
            return pltpu.make_async_copy(src, dst, w_recv.at[y])

        return here, near, far

    def w_start():
        for s in range(2):
            for i in range(2):
                here, near, far = w_pair(s, i)

                @pl.when(here)
                def _():
                    near().start()

                @pl.when(jnp.logical_not(here))
                def _():
                    far().start()

    def w_sent():
        for s in range(2):
            for i in range(2):
                here, near, far = w_pair(s, i)

                @pl.when(jnp.logical_not(here))
                def _():
                    far().wait_send()

    def w_share(i):
        ref = (wup, wdn)[i]
        return remote(ref, ref, ws_send.at[0], ws_recv.at[0], at(cc=1 - c))

    def w_pass():
        @pl.when(c == 0)
        def _():
            for yy in range(NY):
                pltpu.make_async_copy(wup_ref.at[0], wup.at[:, yy * group : (yy + 1) * group], w_recv.at[yy]).wait()
            w_share(0).start()

        @pl.when(c == 1)
        def _():
            for yy in range(NY):
                pltpu.make_async_copy(wdn_ref.at[0], wdn.at[yy * group : (yy + 1) * group], w_recv.at[yy]).wait()
            w_share(1).start()

    def w_done():
        @pl.when(c == 0)
        def _():
            w_share(1).wait_recv()
            w_share(0).wait_send()

        @pl.when(c == 1)
        def _():
            w_share(0).wait_recv()
            w_share(1).wait_send()

    w_start()
    inbound[3].wait()
    fill(1, cot_ref[...])

    middle = chunk // 2
    halves = (pl.ds(0, middle), pl.ds(middle, middle))

    def x_copy(k, s, way, step, mine=True):
        if step == 0:
            block = xbuf.at[k, s, x if mine else (left if way == 0 else right)]
        elif way == 0:
            block = xbuf.at[k, s, left if mine else across, halves[0]]
        else:
            block = xbuf.at[k, s, right if mine else across, halves[1]]
        return remote(
            block, block, x_send.at[k, s, way, step], x_recv.at[k, s, way, step],
            at(xx=right if way == 0 else left),
        )

    def to_x(k, s):
        z_wait(k, s)
        moved = dot(to_rows[...], zbuf[k, s].reshape(chunk * quarters, lanes)).astype(BF16)
        xbuf[k, s, x] = spread(moved)
        x_copy(k, s, 0, 0).start()
        x_copy(k, s, 1, 0).start()

    def pass_on(k, s):
        for way in range(2):
            x_copy(k, s, way, 0, False).wait_recv()
            x_copy(k, s, way, 1).start()

    def last_x(k, s):
        for way in range(2):
            x_copy(k, s, way, 1, False).wait_recv()

    def x_sent(k, s):
        for way in range(2):
            for step in range(2):
                x_copy(k, s, way, step).wait_send()

    half_width = wup.shape[1] // 2

    def forward(s, b):
        block = xbuf[0, s, b]
        value, grad = gelu_parts(dot(block, wup[...]))
        slope[s, b] = grad
        hidden = value.astype(BF16)
        for h in range(2):
            hid[h, s, b] = hidden[:, h * half_width : (h + 1) * half_width]
        part[s, b] = dot(hidden, wdn[...]).astype(BF16)

    def backward(s, b):
        block = xbuf[1, s, b]
        grad = (dot(block, wdn[...], ((1,), (1,))) * slope[s, b]).astype(BF16)
        for h in range(2):
            hg[h, s, b] = grad[:, h * half_width : (h + 1) * half_width]

    def rs_copy(s, d):
        xx = (x + d) % NX
        return remote(part.at[s, xx], rsbuf.at[s, d - 1], rs_send.at[s, d], rs_recv.at[s, d], at(xx=xx))

    def rs_sent(s):
        for d in range(1, NX):
            rs_copy(s, d).wait_send()

    def return_z(s):
        total = part[s, x].astype(F32)
        for d in (1, 3, 2):
            rs_copy(s, d).wait_recv()
            total = total + rsbuf[s, d - 1].astype(F32)
        moved = dot(to_msgs[...], stacked(total.astype(BF16))).astype(BF16)
        zsend[s] = moved.reshape(count, message, lanes)
        zr_start(s)

    everything = 2 * NX * chunk

    def grad_up(h):
        return dot(xbuf[0].reshape(everything, width), hg[h].reshape(everything, half_width), ((0,), (0,)))

    def grad_down(h):
        return dot(hid[h].reshape(everything, half_width), xbuf[1].reshape(everything, width), ((0,), (0,)))

    swap_up = remote(gs_up, gr_up, g_send.at[0], g_recv.at[0], at(cc=1 - c))
    swap_dn = remote(gs_dn, gr_dn, g_send.at[1], g_recv.at[1], at(cc=1 - c))
    owner, mine = y // 2, y % 2

    def gy_pair(k, i):
        yy = 2 * c + k
        src, dst = ((gy_up.at[k], gf_up.at[mine]), (gy_dn.at[k], gf_dn.at[mine]))[i]

        def far():
            return remote(src, dst, gy_send.at[k, i], gy_recv.at[mine, i], at(yy=yy, cc=owner))

        def near():
            return pltpu.make_async_copy(src, dst, gy_recv.at[mine, i])

        return yy == y, near, far

    def gy_start(i):
        for k in range(2):
            here, near, far = gy_pair(k, i)

            @pl.when(here)
            def _():
                near().start()

            @pl.when(jnp.logical_not(here))
            def _():
                far().start()

    def gy_sent(i):
        for k in range(2):
            here, near, far = gy_pair(k, i)

            @pl.when(jnp.logical_not(here))
            def _():
                far().wait_send()

    def gy_wait(i):
        src, dst = ((gy_up, gf_up), (gy_dn, gf_dn))[i]
        for s in range(2):
            pltpu.make_async_copy(src.at[0], dst.at[s], gy_recv.at[s, i]).wait()

    def head():
        zr_wait()
        expert_out = spread(dot(ext_ref[...], zret[...].reshape(slots * quarters, lanes)).astype(BF16))
        field = tok_ref[...].astype(F32) + expert_out.astype(F32)
        inbound[4].wait()
        inbound[5].wait()
        logits = lax.dot_general(
            head_ref[...], field, (((1,), (1,)), ((), ())), precision=lax.Precision.HIGHEST, preferred_element_type=F32
        )
        positive = jnp.maximum(logits, 0.0) + jnp.log1p(jnp.exp(-jnp.abs(logits))) + 0.1
        fine_ref[...] = mass_ref[...] * positive / jnp.sum(positive, axis=0, keepdims=True)

    def forward_near(s):
        forward(s, right)
        rs_copy(s, 1).start()
        forward(s, left)
        rs_copy(s, 3).start()

    def forward_far(s):
        forward(s, across)
        rs_copy(s, 2).start()

    prepare()
    to_x(0, 1)
    w_pass()
    pass_on(0, 1)
    w_done()
    forward(1, x)
    z_sent(0, 1)
    z_sent(0, 0)
    z_start(1, 1)
    z_start(1, 0)
    forward_near(1)
    to_x(0, 0)
    last_x(0, 1)
    forward_far(1)
    forward(0, x)
    pass_on(0, 0)
    forward_near(0)
    to_x(1, 1)
    return_z(1)
    last_x(0, 0)
    forward_far(0)
    backward(1, x)
    pass_on(1, 1)
    to_x(1, 0)
    backward(1, right)
    backward(1, left)
    return_z(0)
    last_x(1, 1)
    backward(1, across)
    backward(0, x)
    pass_on(1, 0)
    backward(0, right)
    backward(0, left)
    last_x(1, 0)
    gs_dn[...] = grad_down(1 - c)
    swap_dn.start()
    backward(0, across)
    gs_up[...] = grad_up(1 - c)
    swap_up.start()
    down = grad_down(c)
    swap_dn.wait_recv()
    down = (down + gr_dn[...]).astype(BF16)
    for k in range(2):
        gy_dn[k] = down[k * group : (k + 1) * group]
    gy_start(1)
    up = grad_up(c)
    swap_up.wait_recv()
    up = (up + gr_up[...]).astype(BF16)
    for k in range(2):
        gy_up[k] = up[:, k * group : (k + 1) * group]
    gy_start(0)
    head()
    gy_wait(1)
    gy_wait(0)

    for s in range(2):
        z_sent(1, s)
        z_sent(2, s)
        for k in range(2):
            x_sent(k, s)
        rs_sent(s)
    swap_up.wait_send()
    swap_dn.wait_send()
    gy_sent(0)
    gy_sent(1)
    w_sent()


def local(
    tokens, cotangent, labels, placement, mass, w_head, w_up, w_down,
    up_moment, up_square, down_moment, down_square,
):
    count, width = tokens.shape
    group = w_up.shape[2]
    full = NY * group
    slots = NZ * NY * CAP
    messages = SET * NY
    chunk = messages * CAP
    lanes = 128
    quarters = width // lanes
    message = quarters * CAP
    vmem = pl.BlockSpec(memory_space=pltpu.VMEM)
    hbm = pl.BlockSpec(memory_space=pl.ANY)
    dma = pltpu.SemaphoreType.DMA
    shape = jax.ShapeDtypeStruct
    pixels, experts = w_head.shape[1], placement.shape[0]
    fine, grad_up, grad_down = pl.pallas_call(
        kernel,
        out_shape=(shape((pixels, count), F32), shape(w_up.shape, BF16), shape(w_down.shape, BF16)),
        in_specs=[hbm] * 8,
        out_specs=[vmem] * 3,
        scratch_shapes=[
            pltpu.VMEM((count, width), BF16),
            pltpu.VMEM((count, width), BF16),
            pltpu.VMEM((1, count), jnp.int32),
            pltpu.VMEM((1, experts), jnp.int32),
            pltpu.VMEM((1, count), F32),
            pltpu.VMEM((pixels, width), F32),
            pltpu.VMEM((slots * quarters, count * quarters), BF16),
            pltpu.VMEM((count * quarters, slots * quarters), BF16),
            pltpu.VMEM((chunk * quarters, chunk * quarters), BF16),
            pltpu.VMEM((chunk * quarters, chunk * quarters), BF16),
            pltpu.VMEM((2, NZ * NY, message, lanes), BF16),
            pltpu.VMEM((2, 2, messages, message, lanes), BF16),
            pltpu.VMEM((2, 2, NX, chunk, width), BF16),
            pltpu.VMEM((width, full), BF16),
            pltpu.VMEM((full, width), BF16),
            pltpu.VMEM((2, 2, NX, chunk, full // 2), BF16),
            pltpu.VMEM((2, NX, chunk, full), F32),
            pltpu.VMEM((2, 2, NX, chunk, full // 2), BF16),
            pltpu.VMEM((2, NX, chunk, width), BF16),
            pltpu.VMEM((2, NX - 1, chunk, width), BF16),
            pltpu.VMEM((2, messages, message, lanes), BF16),
            pltpu.VMEM((NZ * NY, message, lanes), BF16),
            pltpu.VMEM((width, full // 2), F32),
            pltpu.VMEM((full // 2, width), F32),
            pltpu.VMEM((width, full // 2), F32),
            pltpu.VMEM((full // 2, width), F32),
            pltpu.VMEM((2, width, group), BF16),
            pltpu.VMEM((2, group, width), BF16),
            dma((6,)),
            dma((2, 2)), dma((NY,)),
            dma((1,)), dma((1,)),
            dma((3, 2)), dma((3, 2)),
            dma((2, 2, 2, 2)), dma((2, 2, 2, 2)),
            dma((2, NX)), dma((2, NX)),
            dma((2,)), dma((2,)),
            dma((2, 2)), dma((2, 2)),
        ],
        compiler_params=pltpu.CompilerParams(
            collective_id=0, has_side_effects=True, vmem_limit_bytes=56 * 1024 * 1024
        ),
    )(tokens, cotangent, labels.reshape(1, count), placement[None, :], mass[None, :], jnp.transpose(w_head), w_up, w_down)
    up = adam_step(w_up, up_moment, up_square, grad_up.astype(F32))
    down = adam_step(w_down, down_moment, down_square, grad_down.astype(F32))
    return jnp.transpose(fine), up[0], down[0], up[1], up[2], down[1], down[2]


def solution(mesh):
    by_token = P(("dp", "expert"), None)
    up, down = P("expert", None, "dp"), P("expert", "dp", None)
    return jax.shard_map(
        local,
        mesh=mesh,
        in_specs=(
            by_token, by_token, by_token, P(), P(("dp", "expert")), P(),
            up, down, up, up, down, down,
        ),
        out_specs=(by_token, up, down, up, up, down, down),
        check_vma=False,
    )
```
